256 devices in a mesh: pipe: 8 (over y, x_lo), expert: 32 (over z, x_hi, core).
Axes of the slice: x: 4 (x_hi: 2, x_lo: 2; x = x_hi * 2 + x_lo), y: 4, z: 8, core: 2. Of those that a mesh axis runs over, the one named last changes fastest.
Arguments:
- forward_input: bfloat16 [8, 4096, 3584], P('pipe', 'expert'), may hold values from -6 to 6
- forward_route: int32 [8, 4096, 1], P('pipe', 'expert'), may hold values from 0 to 7; in each aligned block of 128 rows (0 to 127, 128 to 255, ..., all dimensions but the last counted through in order) at most 32 rows name the same one
- forward_weight: float32 [8, 4096], P('pipe', 'expert'), may hold values from 0.2 to 1
- section_gradient: bfloat16 [8, 4096, 3584], P('pipe', 'expert'), may hold values from -6 to 6
- backward_route: int32 [8, 4096, 1], P('pipe', 'expert'), may hold values from 0 to 7; in each aligned block of 128 rows (0 to 127, 128 to 255, ..., all dimensions but the last counted through in order) at most 32 rows name the same one
- backward_weight: float32 [8, 4096], P('pipe', 'expert'), may hold values from 0.2 to 1
- saved_gate: bfloat16 [8, 32, 32, 32, 256], P('pipe', 'expert'), may hold values from -6 to 6
- saved_up: bfloat16 [8, 32, 32, 32, 256], P('pipe', 'expert'), may hold values from -6 to 6
- gate_weight: bfloat16 [8, 32, 3584, 256], P('pipe', 'expert'), may hold values from -0.09375 to 0.09375
- up_weight: bfloat16 [8, 32, 3584, 256], P('pipe', 'expert'), may hold values from -0.09375 to 0.09375
- down_weight: bfloat16 [8, 32, 256, 3584], P('pipe', 'expert'), may hold values from -0.1875 to 0.1875
Outputs:
- forward_output: bfloat16 [8, 4096, 3584], P('pipe', 'expert')
- input_gradient: bfloat16 [8, 4096, 3584], P('pipe', 'expert')
- weight_gradient: float32 [8, 4096], P('pipe', 'expert')
The draws below stay inside these ranges and needn't reach their ends.
Inputs may be any that keep to these rules, and one draw needn't show every extreme that they name: `forward_route`: in each device's block of 128 tokens no expert is named by more than 32 tokens, a bound that some block reaches. `backward_route`: in each device's block of 128 tokens no expert is named by more than 32 tokens, a bound that some block reaches.
All inputs are finite; a program needn't handle non-finite values.
Results may differ from the reference program's by a relative error of at most 0.012.
Values may be sent and summed in bfloat16 or wider, within the bound.
No kernel may reach another device: no remote copies, remote signals or barrier semaphores. Data moves between devices by JAX's collectives and lax.ppermute only.
A program may use at most 128 MiB of HBM per device.

```python
import math
import jax
import jax.numpy as jnp
import numpy as np
from jax import lax

D = 3584
FF = 1024
WS = 4
TOPK = 1
TOK_DEV = 128
SECTIONS = 8
SLICES = 32
EXPERTS = 8
FF_DEV = 256
CAP = 32
TOKENS = 4096


def block_levels(rng, dims, split, least, largest):
    factor_of, own = 1.0, jax.random.fold_in(rng, 6)
    for dim, shards_of in split:
        steps = jnp.exp(jax.random.uniform(jax.random.fold_in(own, dim), (shards_of,), jnp.float32, least / len(split), largest / len(split)))
        factor_of = factor_of * jnp.repeat(steps, dims[dim] // shards_of).reshape([-1 if axis == dim else 1 for axis in range(len(dims))])
    return factor_of


def shared_out(own_key, own, number, rows, count, top, limit, skew):
    ranking = jax.random.permutation(own_key, count)
    heavy_load, ordinary = load_shares(count, rows * top, limit, skew, True), load_shares(count, rows * top, limit, skew, False)
    places = jnp.arange(count)

    def named(lengths, offset_by):
        used = int((lengths > 0).sum())
        fixed = max(1, used // 4)
        moved = fixed + (places - fixed + offset_by * (used - fixed)) % max(1, count - fixed)
        return jnp.zeros((count,), jnp.int32).at[ranking[jnp.where(places < fixed, places, moved)]].set(jnp.asarray(lengths, jnp.int32))

    lengths = jnp.where(number % 4 == 0, named(heavy_load, number // 4), named(ordinary, number - number // 4 - 1))
    mixed = jax.random.permutation(jax.random.fold_in(own, 3), count)
    donor, receiver = mixed[0:count // 2 * 2:2], mixed[1:count // 2 * 2:2]
    slack = jnp.minimum(lengths[donor] - 1, limit - lengths[receiver]) // 2
    slack = jnp.where((donor == ranking[0]) | (receiver == ranking[0]) | (lengths[receiver] == 0), 0, jnp.maximum(slack, 0))
    moved = jax.random.randint(jax.random.fold_in(own, 4), (count // 2,), 0, 1 << 20) % (slack + 1)
    lengths = lengths.at[donor].add(-moved).at[receiver].add(moved)
    items = jnp.searchsorted(jnp.cumsum(lengths), jnp.arange(rows * top), side="right").astype(jnp.int32)
    table = items.reshape(top, rows).T
    table = table[jax.random.permutation(jax.random.fold_in(own, 1), rows)]
    offset_by = jax.random.randint(jax.random.fold_in(own, 2), (rows, 1), 0, top)
    return jnp.take_along_axis(table, (jnp.arange(top)[None, :] + offset_by) % top, axis=1)


def load_shares(amount, total, limit, skew, full):
    weights = [(1 << 20) // math.isqrt(standing ** skew) + 1 for standing in range(1, amount + 1)]
    largest = limit if full else min(limit, max(-(-total // amount), total * weights[0] // sum(weights)))
    least = 1 if total - largest >= amount - 1 else 0
    holding, spare = [largest] + [least] * (amount - 1), total - largest - least * (amount - 1)
    while spare > 0:
        candidates = [i for i in range(1, amount) if holding[i] < largest] or [i for i in range(1, amount) if holding[i] < limit]
        mass, budget = sum([weights[i] for i in candidates]), spare
        for i in candidates:
            extra = min(limit - holding[i], max(1, budget * weights[i] // mass), spare)
            holding[i] = holding[i] + extra
            spare = spare - extra
    return np.array(holding)


def centred(key, shape, spread, reach, pieces=(), kind=jnp.bfloat16):
    factor_of = block_levels(key, shape, pieces, -0.22, 0.18) if pieces else 1.0
    drawn = jax.random.normal(key, shape, jnp.float32) * spread * factor_of
    return jnp.minimum(jnp.maximum(drawn, -reach), reach).astype(kind)


def setup_inputs(seed: int = 0) -> dict:
    key_of = jax.random.split(jax.random.key(seed), 12)
    forward_input = centred(key_of[0], (SECTIONS, TOKENS, D), 1.0, 6.0, ((0, 8), (1, 32)))
    forward_route_keys = jax.random.split(jax.random.fold_in(key_of[1], 1), SECTIONS * TOKENS // TOK_DEV)
    forward_route_turns = jax.random.permutation(jax.random.fold_in(key_of[1], 3), SECTIONS * TOKENS // TOK_DEV)
    forward_route = jax.vmap(lambda own, number: shared_out(jax.random.fold_in(key_of[1], 2), own, number, TOK_DEV, EXPERTS, TOPK, CAP, 2))(forward_route_keys, forward_route_turns).reshape((SECTIONS, TOKENS, TOPK))
    forward_weight = jnp.clip(0.2 + 0.8 * jax.random.uniform(key_of[2], (SECTIONS, TOKENS), jnp.float32) ** block_levels(key_of[2], (SECTIONS, TOKENS), ((0, 8), (1, 32)), -0.2, 0.2), 0.2, 1.0)
    section_gradient = centred(key_of[3], (SECTIONS, TOKENS, D), 1.0, 6.0, ((0, 8), (1, 32)))
    backward_route_keys = jax.random.split(jax.random.fold_in(key_of[4], 1), SECTIONS * TOKENS // TOK_DEV)
    backward_route_turns = jax.random.permutation(jax.random.fold_in(key_of[4], 3), SECTIONS * TOKENS // TOK_DEV)
    backward_route = jax.vmap(lambda own, number: shared_out(jax.random.fold_in(key_of[4], 2), own, number, TOK_DEV, EXPERTS, TOPK, CAP, 2))(backward_route_keys, backward_route_turns).reshape((SECTIONS, TOKENS, TOPK))
    backward_weight = jnp.clip(0.2 + 0.8 * jax.random.uniform(key_of[5], (SECTIONS, TOKENS), jnp.float32) ** block_levels(key_of[5], (SECTIONS, TOKENS), ((0, 8), (1, 32)), -0.2, 0.2), 0.2, 1.0)
    saved_gate = centred(key_of[6], (SECTIONS, SLICES, SLICES, CAP, FF_DEV), 1.0, 6.0, ((0, 8), (1, 32)))
    saved_up = centred(key_of[7], (SECTIONS, SLICES, SLICES, CAP, FF_DEV), 1.0, 6.0, ((0, 8), (1, 32)))
    gate_weight = centred(key_of[8], (SECTIONS, SLICES, D, FF_DEV), D ** -0.5, 0.09375, ((0, 8), (1, 32)))
    up_weight = centred(key_of[9], (SECTIONS, SLICES, D, FF_DEV), D ** -0.5, 0.09375, ((0, 8), (1, 32)))
    down_weight = centred(key_of[10], (SECTIONS, SLICES, FF_DEV, D), FF ** -0.5, 0.1875, ((0, 8), (1, 32)))
    return {"forward_input": forward_input, "forward_route": forward_route, "forward_weight": forward_weight, "section_gradient": section_gradient, "backward_route": backward_route, "backward_weight": backward_weight, "saved_gate": saved_gate, "saved_up": saved_up, "gate_weight": gate_weight, "up_weight": up_weight, "down_weight": down_weight}


def slot_index(routes):
    blocks = routes.reshape(SLICES, TOK_DEV).astype(jnp.int32)
    labels = jnp.arange(EXPERTS, dtype=jnp.int32)
    onehot = (blocks[:, :, None] == labels[None, None, :]).astype(jnp.int32)
    before = (jnp.cumsum(onehot, axis=1) - onehot).astype(jnp.int32)
    within = jnp.sum(before * onehot, axis=2).astype(jnp.int32)
    source = jnp.arange(SLICES, dtype=jnp.int32)[:, None]
    flat = (blocks * SLICES + source) * CAP + within
    return flat.reshape(TOKENS).astype(jnp.int32)


def forward_section(inputs, routes, affinity, gates, uppers, downs):
    rows = slot_index(routes)
    buffer = jnp.zeros((EXPERTS * SLICES * CAP, D), jnp.bfloat16).at[rows].set(inputs)
    buffer = buffer.reshape(EXPERTS, SLICES * CAP, D)

    def per_expert(operands):
        block, gate_set, upper_set, down_set = operands
        total = jnp.zeros((SLICES * CAP, D), jnp.float32)
        for shard in range(WS):
            gate = jnp.dot(block, gate_set[shard], preferred_element_type=jnp.float32)
            upper = jnp.dot(block, upper_set[shard], preferred_element_type=jnp.float32)
            hidden = (gate * jax.nn.sigmoid(gate) * upper).astype(jnp.bfloat16)
            part = jnp.dot(hidden, down_set[shard], preferred_element_type=jnp.float32).astype(jnp.bfloat16)
            total = total + part.astype(jnp.float32)
        return total

    summed = lax.map(per_expert, (buffer, gates.reshape(EXPERTS, WS, D, FF_DEV),
                                  uppers.reshape(EXPERTS, WS, D, FF_DEV), downs.reshape(EXPERTS, WS, FF_DEV, D)))
    mixed = summed.reshape(EXPERTS * SLICES * CAP, D)[rows]
    return (inputs.astype(jnp.float32) + affinity[:, None] * mixed).astype(jnp.bfloat16)


def backward_section(upstream, routes, affinity, saved_g, saved_u, gates, uppers, downs):
    rows = slot_index(routes)
    buffer = jnp.zeros((EXPERTS * SLICES * CAP, D), jnp.bfloat16).at[rows].set(upstream)
    buffer = buffer.reshape(EXPERTS, SLICES * CAP, D)

    def per_expert(operands):
        block, gate_pre, upper_pre, gate_set, upper_set, down_set = operands
        total = jnp.zeros((SLICES * CAP, D), jnp.float32)
        shares = jnp.zeros((SLICES * CAP,), jnp.float32)
        for shard in range(WS):
            back_r = jnp.dot(block, down_set[shard].T, preferred_element_type=jnp.float32)
            gate = gate_pre[shard].astype(jnp.float32)
            upper = upper_pre[shard].astype(jnp.float32)
            sigma = jax.nn.sigmoid(gate)
            active = gate * sigma
            saved_hidden = (active * upper).astype(jnp.bfloat16)
            shares = shares + jnp.sum(back_r * saved_hidden.astype(jnp.float32), axis=1)
            d_gate = (back_r * upper * sigma * (1.0 + gate * (1.0 - sigma))).astype(jnp.bfloat16)
            d_up = (back_r * active).astype(jnp.bfloat16)
            back_part = jnp.dot(d_gate, gate_set[shard].T, preferred_element_type=jnp.float32)
            back_part = back_part + jnp.dot(d_up, upper_set[shard].T, preferred_element_type=jnp.float32)
            total = total + back_part.astype(jnp.bfloat16).astype(jnp.float32)
        return total, shares

    summed, shares = lax.map(per_expert, (buffer,
                                          saved_g.reshape(EXPERTS, WS, SLICES * CAP, FF_DEV),
                                          saved_u.reshape(EXPERTS, WS, SLICES * CAP, FF_DEV),
                                          gates.reshape(EXPERTS, WS, D, FF_DEV),
                                          uppers.reshape(EXPERTS, WS, D, FF_DEV),
                                          downs.reshape(EXPERTS, WS, FF_DEV, D)))
    mixed = summed.reshape(EXPERTS * SLICES * CAP, D)[rows]
    weight_terms = shares.reshape(EXPERTS * SLICES * CAP)[rows]
    result = (upstream.astype(jnp.float32) + affinity[:, None] * mixed).astype(jnp.bfloat16)
    return result, weight_terms


def reference(forward_input, forward_route, forward_weight, section_gradient, backward_route, backward_weight,
              saved_gate, saved_up, gate_weight, up_weight, down_weight):
    outputs = []
    gradients = []
    affinity_grads = []
    for layer_index in range(SECTIONS):
        previous = (layer_index - 1) % SECTIONS
        following = (layer_index + 1) % SECTIONS
        outputs.append(forward_section(forward_input[previous], forward_route[layer_index, :, 0],
                                     forward_weight[layer_index], gate_weight[layer_index],
                                     up_weight[layer_index], down_weight[layer_index]))
        result, weight_terms = backward_section(section_gradient[following], backward_route[layer_index, :, 0],
                                              backward_weight[layer_index], saved_gate[layer_index],
                                              saved_up[layer_index], gate_weight[layer_index],
                                              up_weight[layer_index], down_weight[layer_index])
        gradients.append(result)
        affinity_grads.append(weight_terms)
    return (jnp.stack(outputs), jnp.stack(gradients), jnp.stack(affinity_grads))
```

```python
import jax
import jax.numpy as jnp
from jax import lax
from jax.sharding import PartitionSpec as P

WS = 4
AXES = ("pipe", "expert")


def places(index, slices):
    section, place = divmod(index, slices)
    return section, place // WS, place // 2 % 2, place % 2


def send(value, to):
    sections, slices = lax.axis_size("pipe"), lax.axis_size("expert")
    planes = slices // WS
    pairs = []
    for index in range(sections * slices):
        section, plane, half, core = to(*places(index, slices))
        target = (section % sections) * slices + (plane % planes) * WS + half * 2 + core
        pairs.append((index, target))
    return lax.ppermute(value, AXES, pairs)


def shift(value, by):
    return send(value, lambda s, z, h, c: (s + by, z, h, c))


def along(value, by):
    return send(value, lambda s, z, h, c: (s, z + by, h, c))


def swap_half(value):
    return send(value, lambda s, z, h, c: (s, z, 1 - h, c))


def swap_core(value):
    return send(value, lambda s, z, h, c: (s, z, h, 1 - c))


def dot(a, b):
    return jnp.dot(a, b, preferred_element_type=jnp.float32)


def dot_last(a, b):
    return lax.dot_general(a, b, (((1,), (1,)), ((), ())), preferred_element_type=jnp.float32)


def keys_of(routes, plane, planes, capacity):
    labels = jnp.arange(planes, dtype=jnp.int32)
    onehot = (routes[:, None] == labels[None, :]).astype(jnp.int32)
    before = jnp.cumsum(onehot, axis=0) - onehot
    within = jnp.sum(before * onehot, axis=1)
    return (routes - plane + planes) % planes * capacity + within


def pack(values, keys, slots):
    onehot = (jnp.arange(slots, dtype=jnp.int32)[:, None] == keys[None, :]).astype(jnp.bfloat16)
    return dot(onehot, values).astype(jnp.bfloat16)


def unpack(rows, keys):
    onehot = (keys[:, None] == jnp.arange(rows.shape[0], dtype=jnp.int32)[None, :]).astype(jnp.bfloat16)
    return dot(onehot, rows)


def spread(rows, planes, capacity, sign):
    parts = [rows[d * capacity:(d + 1) * capacity] for d in range(planes)]
    return jnp.concatenate([parts[0]] + [along(parts[d], sign * d) for d in range(1, planes)], axis=0)


def per_device(
    forward_input,
    forward_route,
    forward_weight,
    section_gradient,
    backward_route,
    backward_weight,
    saved_gate,
    saved_up,
    gate_weight,
    up_weight,
    down_weight,
):
    slices = lax.axis_size("expert")
    planes = slices // WS
    capacity = saved_gate.shape[3]
    slots = planes * capacity
    place = lax.axis_index("expert")
    plane, half, core = place // WS, place // 2 % 2, place % 2

    inputs = shift(forward_input[0], 1)
    gate_own, up_own, down_own = gate_weight[0, 0], up_weight[0, 0], down_weight[0, 0]

    forward_keys = keys_of(forward_route[0, :, 0], plane, planes, capacity)
    backward_keys = keys_of(backward_route[0, :, 0], plane, planes, capacity)

    gate_next, up_next, down_next = swap_core(gate_own), swap_core(up_own), swap_core(down_own)
    turns = (plane - jnp.arange(planes, dtype=jnp.int32) + planes) % planes * WS
    mine = jnp.concatenate([turns + half * 2 + core, turns + (1 - half) * 2 + core])
    other = jnp.concatenate([turns + half * 2 + 1 - core, turns + (1 - half) * 2 + 1 - core])
    saved_own, saved_next = [], []
    for saved in (saved_gate[0, 0], saved_up[0, 0]):
        saved_own.append(saved[mine].reshape(2 * slots, -1))
        saved_next.append(swap_core(saved[other].reshape(2 * slots, -1)))
    g = jnp.concatenate([saved_own[0], saved_next[0]], axis=1)
    u = jnp.concatenate([saved_own[1], saved_next[1]], axis=1)

    forward_rows = spread(pack(inputs, forward_keys, slots), planes, capacity, 1)

    gradient, down_first, inputs = lax.optimization_barrier((section_gradient[0], down_own, inputs))
    upstream = shift(gradient, -1)
    down_far = swap_half(down_first)
    down_far_next = swap_core(down_far)
    down = jnp.concatenate([down_own, down_next, down_far, down_far_next], axis=0)
    near = down.shape[0] // 2

    def hidden_of(rows):
        parts = []
        for gates, uppers in ((gate_own, up_own), (gate_next, up_next)):
            gate, upper = dot(rows, gates), dot(rows, uppers)
            parts.append((gate * jax.nn.sigmoid(gate) * upper).astype(jnp.bfloat16))
        return jnp.concatenate(parts, axis=1)

    far_rows = swap_half(forward_rows)
    far_hidden = swap_half(hidden_of(far_rows))
    hidden = jnp.concatenate([hidden_of(forward_rows), far_hidden], axis=1)
    returned = spread(dot(hidden, down).astype(jnp.bfloat16), planes, capacity, -1)
    mixed = unpack(returned, forward_keys)
    forward_output = (inputs.astype(jnp.float32) + forward_weight[0][:, None] * mixed).astype(jnp.bfloat16)

    backward_rows = spread(pack(upstream, backward_keys, slots), planes, capacity, 1)
    back_far = swap_half(dot_last(backward_rows, down[near:]).astype(jnp.bfloat16))
    back_near = dot_last(backward_rows, down[:near])

    def back_of(back_r, gate, upper):
        gate, upper = gate.astype(jnp.float32), upper.astype(jnp.float32)
        sigma = jax.nn.sigmoid(gate)
        active = gate * sigma
        saved_hidden = (active * upper).astype(jnp.bfloat16).astype(jnp.float32)
        share = jnp.sum(back_r * saved_hidden, axis=1)
        d_gate = (back_r * upper * sigma * (1.0 + gate * (1.0 - sigma))).astype(jnp.bfloat16)
        d_up = (back_r * active).astype(jnp.bfloat16)
        width = gate_own.shape[1]
        part = dot_last(d_gate[:, :width], gate_own) + dot_last(d_gate[:, width:], gate_next)
        part = part + dot_last(d_up[:, :width], up_own) + dot_last(d_up[:, width:], up_next)
        return part, share

    far_part, far_share = back_of(back_far.astype(jnp.float32), g[slots:], u[slots:])
    far_part = swap_half(far_part.astype(jnp.bfloat16))
    far_share = swap_half(far_share)
    near_part, near_share = back_of(back_near, g[:slots], u[:slots])
    part = (near_part + far_part.astype(jnp.float32)).astype(jnp.bfloat16)
    share = (near_share + far_share).reshape(planes, capacity)
    returned = spread(part, planes, capacity, -1)
    mixed = unpack(returned, backward_keys)
    input_gradient = (upstream.astype(jnp.float32) + backward_weight[0][:, None] * mixed).astype(jnp.bfloat16)
    shares = jnp.concatenate([share[0]] + [along(share[d], -d) for d in range(1, planes)])
    weight_gradient = shares[backward_keys]
    return (forward_output[None], input_gradient[None], weight_gradient[None])


def solution(mesh):
    placed = (
        P("pipe", "expert", None),
        P("pipe", "expert", None),
        P("pipe", "expert"),
        P("pipe", "expert", None),
        P("pipe", "expert", None),
        P("pipe", "expert"),
        P("pipe", "expert", None, None, None),
        P("pipe", "expert", None, None, None),
        P("pipe", "expert", None, None),
        P("pipe", "expert", None, None),
        P("pipe", "expert", None, None),
    )
    return jax.shard_map(
        per_device,
        mesh=mesh,
        in_specs=placed,
        out_specs=(P("pipe", "expert", None), P("pipe", "expert", None), P("pipe", "expert")),
        check_vma=False,
    )
```

```python
import jax
import jax.numpy as jnp
from jax import lax
from jax.sharding import PartitionSpec as P

WS = 4
AXES = ("pipe", "expert")


def places(index, slices):
    section, place = divmod(index, slices)
    return section, place // WS, place // 2 % 2, place % 2


def send(value, to):
    sections, slices = lax.axis_size("pipe"), lax.axis_size("expert")
    planes = slices // WS
    pairs = []
    for index in range(sections * slices):
        section, plane, half, core = to(*places(index, slices))
        target = (section % sections) * slices + (plane % planes) * WS + half * 2 + core
        pairs.append((index, target))
    return lax.ppermute(value, AXES, pairs)


def shift(value, by):
    return send(value, lambda s, z, h, c: (s + by, z, h, c))


def onward(value, by):
    return send(value, lambda s, z, h, c: (s + s % 2 * 2, z + by, h, c))


def across(value, far):
    return send(value, lambda s, z, h, c: (s + 1 - s % 2 * 2, z, h ^ far, c))


def swap_half(value):
    return send(value, lambda s, z, h, c: (s, z, 1 - h, c))


def swap_core(value):
    return send(value, lambda s, z, h, c: (s, z, h, 1 - c))


def dot(a, b):
    return jnp.dot(a, b, preferred_element_type=jnp.float32)


def dot_last(a, b):
    return lax.dot_general(a, b, (((1,), (1,)), ((), ())), preferred_element_type=jnp.float32)


def keys_of(routes, planes, capacity):
    labels = jnp.arange(planes, dtype=jnp.int32)
    onehot = (routes[:, None] == labels[None, :]).astype(jnp.int32)
    before = jnp.cumsum(onehot, axis=0) - onehot
    within = jnp.sum(before * onehot, axis=1)
    return routes * capacity + within


def pack(values, keys, slots):
    onehot = (jnp.arange(slots, dtype=jnp.int32)[:, None] == keys[None, :]).astype(jnp.bfloat16)
    return dot(onehot, values).astype(jnp.bfloat16)


def unpack(rows, keys):
    onehot = (keys[:, None] == jnp.arange(rows.shape[0], dtype=jnp.int32)[None, :]).astype(jnp.bfloat16)
    return dot(onehot, rows)


def exchange(rows, planes):
    groups = [[plane * WS + place for plane in range(planes)] for place in range(WS)]
    return lax.all_to_all(rows, "expert", 0, 0, axis_index_groups=groups, tiled=True)


def per_device(
    forward_input,
    forward_route,
    forward_weight,
    section_gradient,
    backward_route,
    backward_weight,
    saved_gate,
    saved_up,
    gate_weight,
    up_weight,
    down_weight,
):
    slices = lax.axis_size("expert")
    planes = slices // WS
    capacity = saved_gate.shape[3]
    slots = planes * capacity
    place = lax.axis_index("expert")
    half, core = place // 2 % 2, place % 2

    gate_own, up_own, down_own = gate_weight[0, 0], up_weight[0, 0], down_weight[0, 0]
    onward_route = shift(forward_route[0, :, 0], -1)
    upstream = shift(section_gradient[0], -1)

    forward_keys = keys_of(forward_route[0, :, 0], planes, capacity)
    backward_keys = keys_of(backward_route[0, :, 0], planes, capacity)
    plane = place // WS
    onward_keys = keys_of((onward_route - plane + planes) % planes, planes, capacity)
    packed = pack(forward_input[0], onward_keys, slots)
    order = [distance for pair in zip(range(planes // 2, planes), range(planes // 2 - 1, -1, -1)) for distance in pair]
    arrived = {d: onward(packed[d * capacity:(d + 1) * capacity], d) for d in order}
    forward_rows = jnp.concatenate([arrived[d] for d in range(planes)], axis=0)

    turns = jnp.arange(planes, dtype=jnp.int32) * WS
    mine = jnp.concatenate([turns + half * 2 + core, turns + (1 - half) * 2 + core])
    other = jnp.concatenate([turns + half * 2 + 1 - core, turns + (1 - half) * 2 + 1 - core])
    saved = jnp.concatenate([saved_gate[0, 0], saved_up[0, 0]], axis=2)
    saved_own, saved_next = saved[mine].reshape(2 * slots, -1), saved[other].reshape(2 * slots, -1)

    down_far = swap_half(down_own)
    backward_packed = pack(upstream, backward_keys, slots)
    forward_rows, backward_packed, down_far, gate_own, up_own, saved_next, saved_own, forward_first = lax.optimization_barrier(
        (forward_rows, backward_packed, down_far, gate_own, up_own, saved_next, saved_own, forward_input[0])
    )

    far_rows, near_rows = across(forward_rows, 1), across(forward_rows, 0)
    saved_next = swap_core(saved_next)
    saved_next, backward_packed, gate_own, up_own, down_own, down_far = lax.optimization_barrier(
        (saved_next, backward_packed, gate_own, up_own, down_own, down_far)
    )
    backward_rows = exchange(backward_packed, planes)
    gates = jnp.concatenate([gate_own, swap_core(gate_own), up_own, swap_core(up_own)], axis=1)
    down = jnp.concatenate([down_own, swap_core(down_own), down_far, swap_core(down_far)], axis=0)
    near = down.shape[0] // 2
    units = near // 2
    g = jnp.concatenate([saved_own[:, :units], saved_next[:, :units]], axis=1)
    u = jnp.concatenate([saved_own[:, units:], saved_next[:, units:]], axis=1)

    def hidden_of(rows):
        both = dot(rows, gates)
        gate, upper = both[:, :near], both[:, near:]
        return (gate * jax.nn.sigmoid(gate) * upper).astype(jnp.bfloat16)

    far_hidden = hidden_of(far_rows)
    far_hidden, forward_first = lax.optimization_barrier((far_hidden, forward_first))
    far_hidden = swap_half(far_hidden)
    inputs = shift(forward_first, 1)
    hidden = jnp.concatenate([hidden_of(near_rows), far_hidden], axis=1)
    turned = (plane - jnp.arange(planes, dtype=jnp.int32) + planes) % planes
    hidden = jnp.take(hidden.reshape(planes, capacity, -1), turned, axis=0).reshape(slots, -1)
    returned = exchange(dot(hidden, down).astype(jnp.bfloat16), planes)
    mixed = unpack(returned, forward_keys)
    forward_output = (inputs.astype(jnp.float32) + forward_weight[0][:, None] * mixed).astype(jnp.bfloat16)

    back_far = swap_half(dot_last(backward_rows, down[near:]).astype(jnp.bfloat16))
    back_near = dot_last(backward_rows, down[:near])

    def back_of(back_r, gate, upper):
        gate, upper = gate.astype(jnp.float32), upper.astype(jnp.float32)
        sigma = jax.nn.sigmoid(gate)
        active = gate * sigma
        saved_hidden = (active * upper).astype(jnp.bfloat16).astype(jnp.float32)
        share = jnp.sum(back_r * saved_hidden, axis=1)
        d_gate = (back_r * upper * sigma * (1.0 + gate * (1.0 - sigma))).astype(jnp.bfloat16)
        d_up = (back_r * active).astype(jnp.bfloat16)
        return dot_last(jnp.concatenate([d_gate, d_up], axis=1), gates), share

    far_part, far_share = back_of(back_far.astype(jnp.float32), g[slots:], u[slots:])
    far_part = swap_half(far_part.astype(jnp.bfloat16))
    far_share = swap_half(far_share)
    near_part, near_share = back_of(back_near, g[:slots], u[:slots])
    part = (near_part + far_part.astype(jnp.float32)).astype(jnp.bfloat16)
    rest, terms = near_share + far_share, []
    for _ in range(3):
        terms.append(rest.astype(jnp.bfloat16))
        rest = rest - terms[-1].astype(jnp.float32)
    width = part.shape[1]
    column = jnp.arange(128, dtype=jnp.int32)[None, :]
    tail = sum(jnp.where(column == n, term[:, None], jnp.bfloat16(0)) for n, term in enumerate(terms))
    returned = exchange(jnp.concatenate([part, tail], axis=1), planes)
    mixed = unpack(returned, backward_keys)
    weight_gradient = jnp.sum(mixed[:, width:], axis=1)
    mixed = mixed[:, :width]
    input_gradient = (upstream.astype(jnp.float32) + backward_weight[0][:, None] * mixed).astype(jnp.bfloat16)
    return (forward_output[None], input_gradient[None], weight_gradient[None])


def solution(mesh):
    placed = (
        P("pipe", "expert", None),
        P("pipe", "expert", None),
        P("pipe", "expert"),
        P("pipe", "expert", None),
        P("pipe", "expert", None),
        P("pipe", "expert"),
        P("pipe", "expert", None, None, None),
        P("pipe", "expert", None, None, None),
        P("pipe", "expert", None, None),
        P("pipe", "expert", None, None),
        P("pipe", "expert", None, None),
    )
    return jax.shard_map(
        per_device,
        mesh=mesh,
        in_specs=placed,
        out_specs=(P("pipe", "expert", None), P("pipe", "expert", None), P("pipe", "expert")),
        check_vma=False,
    )
```

```python
import jax
import jax.numpy as jnp
from jax import lax
from jax.sharding import PartitionSpec as P

WS = 4
AXES = ("pipe", "expert")


def places(index, slices):
    section, place = divmod(index, slices)
    return section, place // WS, place // 2 % 2, place % 2


def send(value, to):
    sections, slices = lax.axis_size("pipe"), lax.axis_size("expert")
    planes = slices // WS
    pairs = []
    for index in range(sections * slices):
        section, plane, half, core = to(*places(index, slices))
        target = (section % sections) * slices + (plane % planes) * WS + half * 2 + core
        pairs.append((index, target))
    return lax.ppermute(value, AXES, pairs)


def shift(value, by):
    return send(value, lambda s, z, h, c: (s + by, z, h, c))


def onward(value, by):
    return send(value, lambda s, z, h, c: (s + s % 2 * 2, z + by, h, c))


def across(value, far):
    return send(value, lambda s, z, h, c: (s + 1 - s % 2 * 2, z, h ^ far, c))


def swap_half(value):
    return send(value, lambda s, z, h, c: (s, z, 1 - h, c))


def swap_core(value):
    return send(value, lambda s, z, h, c: (s, z, h, 1 - c))


def dot(a, b):
    return jnp.dot(a, b, preferred_element_type=jnp.float32)


def dot_last(a, b):
    return lax.dot_general(a, b, (((1,), (1,)), ((), ())), preferred_element_type=jnp.float32)


def keys_of(routes, planes, capacity):
    labels = jnp.arange(planes, dtype=jnp.int32)
    onehot = (routes[:, None] == labels[None, :]).astype(jnp.int32)
    before = jnp.cumsum(onehot, axis=0) - onehot
    within = jnp.sum(before * onehot, axis=1)
    return routes * capacity + within


def pack(values, keys, slots):
    onehot = (jnp.arange(slots, dtype=jnp.int32)[:, None] == keys[None, :]).astype(jnp.bfloat16)
    return dot(onehot, values).astype(jnp.bfloat16)


def unpack(rows, keys):
    onehot = (keys[:, None] == jnp.arange(rows.shape[0], dtype=jnp.int32)[None, :]).astype(jnp.bfloat16)
    return dot(onehot, rows)


def exchange(rows, planes):
    groups = [[plane * WS + place for plane in range(planes)] for place in range(WS)]
    return lax.all_to_all(rows, "expert", 0, 0, axis_index_groups=groups, tiled=True)


def per_device(
    forward_input,
    forward_route,
    forward_weight,
    section_gradient,
    backward_route,
    backward_weight,
    saved_gate,
    saved_up,
    gate_weight,
    up_weight,
    down_weight,
):
    slices = lax.axis_size("expert")
    planes = slices // WS
    capacity = saved_gate.shape[3]
    slots = planes * capacity
    place = lax.axis_index("expert")
    half, core = place // 2 % 2, place % 2

    gate_own, up_own, down_own = gate_weight[0, 0], up_weight[0, 0], down_weight[0, 0]
    onward_route = shift(forward_route[0, :, 0], -1)
    upstream = shift(section_gradient[0], -1)

    forward_keys = keys_of(forward_route[0, :, 0], planes, capacity)
    backward_keys = keys_of(backward_route[0, :, 0], planes, capacity)
    plane = place // WS
    onward_keys = keys_of((onward_route - plane + planes) % planes, planes, capacity)
    packed = pack(forward_input[0], onward_keys, slots)
    order = [distance for pair in zip(range(planes // 2, planes), range(planes // 2 - 1, -1, -1)) for distance in pair]
    arrived = {d: onward(packed[d * capacity:(d + 1) * capacity], d) for d in order}
    backward_packed, arrived[order[2]] = lax.optimization_barrier(
        (pack(upstream, backward_keys, slots), arrived[order[2]])
    )
    forward_rows = jnp.concatenate([arrived[d] for d in range(planes)], axis=0)

    turns = jnp.arange(planes, dtype=jnp.int32) * WS
    mine = jnp.concatenate([turns + half * 2 + core, turns + (1 - half) * 2 + core])
    other = jnp.concatenate([turns + half * 2 + 1 - core, turns + (1 - half) * 2 + 1 - core])
    saved = jnp.concatenate([saved_gate[0, 0], saved_up[0, 0]], axis=2)
    saved_own, saved_next = saved[mine].reshape(2 * slots, -1), saved[other].reshape(2 * slots, -1)

    down_far = swap_half(down_own)
    gate_first, up_first = gate_own, up_own
    forward_rows, backward_packed, down_far, gate_own, up_own, saved_next, saved_own, forward_first = lax.optimization_barrier(
        (forward_rows, backward_packed, down_far, gate_own, up_own, saved_next, saved_own, forward_input[0])
    )

    far_rows, near_rows = across(forward_rows, 1), across(forward_rows, 0)
    saved_next = swap_core(saved_next)
    saved_next, backward_packed, gate_own, up_own, down_own, down_far = lax.optimization_barrier(
        (saved_next, backward_packed, gate_own, up_own, down_own, down_far)
    )
    backward_rows = exchange(backward_packed, planes)
    gates = jnp.concatenate([gate_first, swap_core(gate_own), up_first, swap_core(up_own)], axis=1)
    down = jnp.concatenate([down_own, swap_core(down_own), down_far, swap_core(down_far)], axis=0)
    near = down.shape[0] // 2
    units = near // 2
    g = jnp.concatenate([saved_own[:, :units], saved_next[:, :units]], axis=1)
    u = jnp.concatenate([saved_own[:, units:], saved_next[:, units:]], axis=1)

    def hidden_of(rows):
        both = dot(rows, gates)
        gate, upper = both[:, :near], both[:, near:]
        return (gate * jax.nn.sigmoid(gate) * upper).astype(jnp.bfloat16)

    far_hidden = hidden_of(far_rows)
    far_hidden, forward_first = lax.optimization_barrier((far_hidden, forward_first))
    far_hidden = swap_half(far_hidden)
    inputs = shift(forward_first, 1)
    hidden = jnp.concatenate([hidden_of(near_rows), far_hidden], axis=1)
    turned = (plane - jnp.arange(planes, dtype=jnp.int32) + planes) % planes
    hidden = jnp.take(hidden.reshape(planes, capacity, -1), turned, axis=0).reshape(slots, -1)
    returned = exchange(dot(hidden, down).astype(jnp.bfloat16), planes)
    mixed = unpack(returned, forward_keys)
    forward_output = (inputs.astype(jnp.float32) + forward_weight[0][:, None] * mixed).astype(jnp.bfloat16)

    back_far = swap_half(dot_last(backward_rows, down[near:]).astype(jnp.bfloat16))

    def back_of(back_r, gate, upper):
        gate, upper = gate.astype(jnp.float32), upper.astype(jnp.float32)
        sigma = jax.nn.sigmoid(gate)
        active = gate * sigma
        saved_hidden = (active * upper).astype(jnp.bfloat16).astype(jnp.float32)
        share = jnp.sum(back_r * saved_hidden, axis=1)
        d_gate = (back_r * upper * sigma * (1.0 + gate * (1.0 - sigma))).astype(jnp.bfloat16)
        d_up = (back_r * active).astype(jnp.bfloat16)
        return jnp.concatenate([d_gate, d_up], axis=1), share

    far_terms, far_share = back_of(back_far.astype(jnp.float32), g[slots:], u[slots:])
    far_terms, backward_rows = lax.optimization_barrier((far_terms, backward_rows))
    far_part = dot_last(far_terms, gates)
    far_part = swap_half(far_part.astype(jnp.bfloat16))
    far_share = swap_half(far_share)
    near_terms, near_share = back_of(dot_last(backward_rows, down[:near]), g[:slots], u[:slots])
    near_part = dot_last(near_terms, gates)
    part = (near_part + far_part.astype(jnp.float32)).astype(jnp.bfloat16)
    rest, terms = near_share + far_share, []
    for _ in range(3):
        terms.append(rest.astype(jnp.bfloat16))
        rest = rest - terms[-1].astype(jnp.float32)
    width = part.shape[1]
    column = jnp.arange(128, dtype=jnp.int32)[None, :]
    tail = sum(jnp.where(column == n, term[:, None], jnp.bfloat16(0)) for n, term in enumerate(terms))
    returned = exchange(jnp.concatenate([part, tail], axis=1), planes)
    mixed = unpack(returned, backward_keys)
    weight_gradient = jnp.sum(mixed[:, width:], axis=1)
    mixed = mixed[:, :width]
    input_gradient = (upstream.astype(jnp.float32) + backward_weight[0][:, None] * mixed).astype(jnp.bfloat16)
    return (forward_output[None], input_gradient[None], weight_gradient[None])


def solution(mesh):
    placed = (
        P("pipe", "expert", None),
        P("pipe", "expert", None),
        P("pipe", "expert"),
        P("pipe", "expert", None),
        P("pipe", "expert", None),
        P("pipe", "expert"),
        P("pipe", "expert", None, None, None),
        P("pipe", "expert", None, None, None),
        P("pipe", "expert", None, None),
        P("pipe", "expert", None, None),
        P("pipe", "expert", None, None),
    )
    return jax.shard_map(
        per_device,
        mesh=mesh,
        in_specs=placed,
        out_specs=(P("pipe", "expert", None), P("pipe", "expert", None), P("pipe", "expert")),
        check_vma=False,
    )
```

```python
import jax
import jax.numpy as jnp
from jax import lax
from jax.sharding import PartitionSpec as P

WS = 4
AXES = ("pipe", "expert")


def places(index, slices):
    section, place = divmod(index, slices)
    return section, place // WS, place // 2 % 2, place % 2


def send(value, to):
    sections, slices = lax.axis_size("pipe"), lax.axis_size("expert")
    planes = slices // WS
    pairs = []
    for index in range(sections * slices):
        section, plane, half, core = to(*places(index, slices))
        target = (section % sections) * slices + (plane % planes) * WS + half * 2 + core
        pairs.append((index, target))
    return lax.ppermute(value, AXES, pairs)


def shift(value, by):
    return send(value, lambda s, z, h, c: (s + by, z, h, c))


def onward(value, by):
    return send(value, lambda s, z, h, c: (s + s % 2 * 2, z + by, h, c))


def across(value, far):
    return send(value, lambda s, z, h, c: (s + 1 - s % 2 * 2, z, h ^ far, c))


def swap_half(value):
    return send(value, lambda s, z, h, c: (s, z, 1 - h, c))


def swap_core(value):
    return send(value, lambda s, z, h, c: (s, z, h, 1 - c))


def dot(a, b):
    return jnp.dot(a, b, preferred_element_type=jnp.float32)


def dot_last(a, b):
    return lax.dot_general(a, b, (((1,), (1,)), ((), ())), preferred_element_type=jnp.float32)


def keys_of(routes, planes, capacity):
    labels = jnp.arange(planes, dtype=jnp.int32)
    onehot = (routes[:, None] == labels[None, :]).astype(jnp.int32)
    before = jnp.cumsum(onehot, axis=0) - onehot
    within = jnp.sum(before * onehot, axis=1)
    return routes * capacity + within


def pack(values, keys, slots):
    onehot = (jnp.arange(slots, dtype=jnp.int32)[:, None] == keys[None, :]).astype(jnp.bfloat16)
    return dot(onehot, values).astype(jnp.bfloat16)


def unpack(rows, keys):
    onehot = (keys[:, None] == jnp.arange(rows.shape[0], dtype=jnp.int32)[None, :]).astype(jnp.bfloat16)
    return dot(onehot, rows)


def exchange(rows, planes):
    groups = [[plane * WS + place for plane in range(planes)] for place in range(WS)]
    return lax.all_to_all(rows, "expert", 0, 0, axis_index_groups=groups, tiled=True)


def per_device(
    forward_input,
    forward_route,
    forward_weight,
    section_gradient,
    backward_route,
    backward_weight,
    saved_gate,
    saved_up,
    gate_weight,
    up_weight,
    down_weight,
):
    slices = lax.axis_size("expert")
    planes = slices // WS
    capacity = saved_gate.shape[3]
    slots = planes * capacity
    place = lax.axis_index("expert")
    half, core = place // 2 % 2, place % 2

    gate_own, up_own, down_own = gate_weight[0, 0], up_weight[0, 0], down_weight[0, 0]
    onward_route = shift(forward_route[0, :, 0], -1)
    upstream = shift(section_gradient[0], -1)

    forward_keys = keys_of(forward_route[0, :, 0], planes, capacity)
    backward_keys = keys_of(backward_route[0, :, 0], planes, capacity)
    plane = place // WS
    onward_keys = keys_of((onward_route - plane + planes) % planes, planes, capacity)
    packed = pack(forward_input[0], onward_keys, slots)
    order = sorted(range(planes), key=lambda d: (d != planes // 2, d != 0, -min(d, planes - d)))
    arrived = {d: onward(packed[d * capacity:(d + 1) * capacity], d) for d in order}
    backward_packed, arrived[order[2]] = lax.optimization_barrier(
        (pack(upstream, backward_keys, slots), arrived[order[2]])
    )
    forward_rows = jnp.concatenate([arrived[d] for d in range(planes)], axis=0)

    turns = jnp.arange(planes, dtype=jnp.int32) * WS
    mine = jnp.concatenate([turns + half * 2 + core, turns + (1 - half) * 2 + core])
    other = jnp.concatenate([turns + half * 2 + 1 - core, turns + (1 - half) * 2 + 1 - core])
    saved = jnp.concatenate([saved_gate[0, 0], saved_up[0, 0]], axis=2)
    saved_own, saved_next = saved[mine].reshape(2 * slots, -1), saved[other].reshape(2 * slots, -1)

    down_far = swap_half(down_own)
    gate_first, up_first = gate_own, up_own
    forward_rows, backward_packed, down_far, gate_own, up_own, saved_next, saved_own, forward_first = lax.optimization_barrier(
        (forward_rows, backward_packed, down_far, gate_own, up_own, saved_next, saved_own, forward_input[0])
    )

    far_rows, near_rows = across(forward_rows, 1), across(forward_rows, 0)
    saved_next = swap_core(saved_next)
    saved_next, backward_packed, gate_own, up_own, down_own, down_far = lax.optimization_barrier(
        (saved_next, backward_packed, gate_own, up_own, down_own, down_far)
    )
    backward_rows = exchange(backward_packed, planes)
    gates = jnp.concatenate([gate_first, swap_core(gate_own), up_first, swap_core(up_own)], axis=1)
    down = jnp.concatenate([down_own, swap_core(down_own), down_far, swap_core(down_far)], axis=0)
    near = down.shape[0] // 2
    units = near // 2
    g = jnp.concatenate([saved_own[:, :units], saved_next[:, :units]], axis=1)
    u = jnp.concatenate([saved_own[:, units:], saved_next[:, units:]], axis=1)

    def hidden_of(rows):
        both = dot(rows, gates)
        gate, upper = both[:, :near], both[:, near:]
        return (gate * jax.nn.sigmoid(gate) * upper).astype(jnp.bfloat16)

    far_hidden = hidden_of(far_rows)
    far_hidden, forward_first = lax.optimization_barrier((far_hidden, forward_first))
    far_hidden = swap_half(far_hidden)
    inputs = shift(forward_first, 1)
    hidden = jnp.concatenate([hidden_of(near_rows), far_hidden], axis=1)
    turned = (plane - jnp.arange(planes, dtype=jnp.int32) + planes) % planes
    hidden = jnp.take(hidden.reshape(planes, capacity, -1), turned, axis=0).reshape(slots, -1)
    returned = exchange(dot(hidden, down).astype(jnp.bfloat16), planes)
    mixed = unpack(returned, forward_keys)
    forward_output = (inputs.astype(jnp.float32) + forward_weight[0][:, None] * mixed).astype(jnp.bfloat16)

    back_far = swap_half(dot_last(backward_rows, down[near:]).astype(jnp.bfloat16))

    def back_of(back_r, gate, upper):
        gate, upper = gate.astype(jnp.float32), upper.astype(jnp.float32)
        sigma = jax.nn.sigmoid(gate)
        active = gate * sigma
        saved_hidden = (active * upper).astype(jnp.bfloat16).astype(jnp.float32)
        share = jnp.sum(back_r * saved_hidden, axis=1)
        d_gate = (back_r * upper * sigma * (1.0 + gate * (1.0 - sigma))).astype(jnp.bfloat16)
        d_up = (back_r * active).astype(jnp.bfloat16)
        return jnp.concatenate([d_gate, d_up], axis=1), share

    far_terms, far_share = back_of(back_far.astype(jnp.float32), g[slots:], u[slots:])
    far_terms, backward_rows = lax.optimization_barrier((far_terms, backward_rows))
    middle = gates.shape[0] // 2
    far_part = jnp.concatenate(
        [swap_half(dot_last(far_terms, rows).astype(jnp.bfloat16)) for rows in (gates[:middle], gates[middle:])], axis=1
    )
    far_share = swap_half(far_share)
    near_terms, near_share = back_of(dot_last(backward_rows, down[:near]), g[:slots], u[:slots])
    near_part = dot_last(near_terms, gates)
    part = (near_part + far_part.astype(jnp.float32)).astype(jnp.bfloat16)
    rest, terms = near_share + far_share, []
    for _ in range(3):
        terms.append(rest.astype(jnp.bfloat16))
        rest = rest - terms[-1].astype(jnp.float32)
    width = part.shape[1]
    column = jnp.arange(128, dtype=jnp.int32)[None, :]
    tail = sum(jnp.where(column == n, term[:, None], jnp.bfloat16(0)) for n, term in enumerate(terms))
    returned = exchange(jnp.concatenate([part, tail], axis=1), planes)
    mixed = unpack(returned, backward_keys)
    weight_gradient = jnp.sum(mixed[:, width:], axis=1)
    mixed = mixed[:, :width]
    input_gradient = (upstream.astype(jnp.float32) + backward_weight[0][:, None] * mixed).astype(jnp.bfloat16)
    return (forward_output[None], input_gradient[None], weight_gradient[None])


def solution(mesh):
    placed = (
        P("pipe", "expert", None),
        P("pipe", "expert", None),
        P("pipe", "expert"),
        P("pipe", "expert", None),
        P("pipe", "expert", None),
        P("pipe", "expert"),
        P("pipe", "expert", None, None, None),
        P("pipe", "expert", None, None, None),
        P("pipe", "expert", None, None),
        P("pipe", "expert", None, None),
        P("pipe", "expert", None, None),
    )
    return jax.shard_map(
        per_device,
        mesh=mesh,
        in_specs=placed,
        out_specs=(P("pipe", "expert", None), P("pipe", "expert", None), P("pipe", "expert")),
        check_vma=False,
    )
```

```python
import jax
import jax.numpy as jnp
from jax import lax
from jax.sharding import PartitionSpec as P

WS = 4
AXES = ("pipe", "expert")


def places(index, slices):
    section, place = divmod(index, slices)
    return section, place // WS, place // 2 % 2, place % 2


def send(value, to):
    sections, slices = lax.axis_size("pipe"), lax.axis_size("expert")
    planes = slices // WS
    pairs = []
    for index in range(sections * slices):
        section, plane, half, core = to(*places(index, slices))
        target = (section % sections) * slices + (plane % planes) * WS + half * 2 + core
        pairs.append((index, target))
    return lax.ppermute(value, AXES, pairs)


def shift(value, by):
    return send(value, lambda s, z, h, c: (s + by, z, h, c))


def onward(value, by):
    return send(value, lambda s, z, h, c: (s + s % 2 * 2, z + by, h, c))


def across(value, far):
    return send(value, lambda s, z, h, c: (s + 1 - s % 2 * 2, z, h ^ far, c))


def swap_half(value):
    return send(value, lambda s, z, h, c: (s, z, 1 - h, c))


def swap_core(value):
    return send(value, lambda s, z, h, c: (s, z, h, 1 - c))


def dot(a, b):
    return jnp.dot(a, b, preferred_element_type=jnp.float32)


def dot_last(a, b):
    return lax.dot_general(a, b, (((1,), (1,)), ((), ())), preferred_element_type=jnp.float32)


def keys_of(routes, planes, capacity):
    labels = jnp.arange(planes, dtype=jnp.int32)
    onehot = (routes[:, None] == labels[None, :]).astype(jnp.int32)
    before = jnp.cumsum(onehot, axis=0) - onehot
    within = jnp.sum(before * onehot, axis=1)
    return routes * capacity + within


def pack(values, keys, slots):
    onehot = (jnp.arange(slots, dtype=jnp.int32)[:, None] == keys[None, :]).astype(jnp.bfloat16)
    return dot(onehot, values).astype(jnp.bfloat16)


def unpack(rows, keys):
    onehot = (keys[:, None] == jnp.arange(rows.shape[0], dtype=jnp.int32)[None, :]).astype(jnp.bfloat16)
    return dot(onehot, rows)


def exchange(rows, planes):
    groups = [[plane * WS + place for plane in range(planes)] for place in range(WS)]
    return lax.all_to_all(rows, "expert", 0, 0, axis_index_groups=groups, tiled=True)


def per_device(
    forward_input,
    forward_route,
    forward_weight,
    section_gradient,
    backward_route,
    backward_weight,
    saved_gate,
    saved_up,
    gate_weight,
    up_weight,
    down_weight,
):
    slices = lax.axis_size("expert")
    planes = slices // WS
    capacity = saved_gate.shape[3]
    slots = planes * capacity
    place = lax.axis_index("expert")
    half, core = place // 2 % 2, place % 2

    gate_own, up_own, down_own = gate_weight[0, 0], up_weight[0, 0], down_weight[0, 0]
    onward_route = shift(forward_route[0, :, 0], -1)
    upstream = shift(section_gradient[0], -1)

    forward_keys = keys_of(forward_route[0, :, 0], planes, capacity)
    backward_keys = keys_of(backward_route[0, :, 0], planes, capacity)
    plane = place // WS
    onward_keys = keys_of((onward_route - plane + planes) % planes, planes, capacity)
    packed = pack(forward_input[0], onward_keys, slots)
    order = sorted(range(planes), key=lambda d: (d != planes // 2, d != 0, -min(d, planes - d)))
    arrived = {d: onward(packed[d * capacity:(d + 1) * capacity], d) for d in order}
    backward_packed, arrived[order[2]] = lax.optimization_barrier(
        (pack(upstream, backward_keys, slots), arrived[order[2]])
    )
    forward_rows = jnp.concatenate([arrived[d] for d in range(planes)], axis=0)

    turns = jnp.arange(planes, dtype=jnp.int32) * WS
    mine = jnp.concatenate([turns + half * 2 + core, turns + (1 - half) * 2 + core])
    other = jnp.concatenate([turns + half * 2 + 1 - core, turns + (1 - half) * 2 + 1 - core])
    saved = jnp.concatenate([saved_gate[0, 0], saved_up[0, 0]], axis=2)
    saved_own, saved_next = saved[mine].reshape(2 * slots, -1), saved[other].reshape(2 * slots, -1)

    down_far = swap_half(down_own)
    gate_first, up_first = gate_own, up_own
    forward_rows, backward_packed, down_far, gate_own, up_own, saved_next, saved_own, forward_first = lax.optimization_barrier(
        (forward_rows, backward_packed, down_far, gate_own, up_own, saved_next, saved_own, forward_input[0])
    )

    far_rows, near_rows = across(forward_rows, 1), across(forward_rows, 0)
    saved_next = swap_core(saved_next)
    saved_next, backward_packed, gate_own, up_own, down_own, down_far = lax.optimization_barrier(
        (saved_next, backward_packed, gate_own, up_own, down_own, down_far)
    )
    backward_rows = exchange(backward_packed, planes)
    gates = jnp.concatenate([gate_first, swap_core(gate_own), up_first, swap_core(up_own)], axis=1)
    down = jnp.concatenate([down_own, swap_core(down_own), down_far, swap_core(down_far)], axis=0)
    near = down.shape[0] // 2
    units = near // 2
    g = jnp.concatenate([saved_own[:, :units], saved_next[:, :units]], axis=1)
    u = jnp.concatenate([saved_own[:, units:], saved_next[:, units:]], axis=1)

    def hidden_of(rows):
        both = dot(rows, gates)
        gate, upper = both[:, :near], both[:, near:]
        return (gate * jax.nn.sigmoid(gate) * upper).astype(jnp.bfloat16)

    far_hidden = hidden_of(far_rows)
    far_hidden, forward_first = lax.optimization_barrier((far_hidden, forward_first))
    far_hidden = swap_half(far_hidden)
    inputs = shift(forward_first, 1)
    hidden = jnp.concatenate([hidden_of(near_rows), far_hidden], axis=1)
    turned = (plane - jnp.arange(planes, dtype=jnp.int32) + planes) % planes
    hidden = jnp.take(hidden.reshape(planes, capacity, -1), turned, axis=0).reshape(slots, -1)
    returned = exchange(dot(hidden, down).astype(jnp.bfloat16), planes)
    mixed = unpack(returned, forward_keys)
    forward_output = (inputs.astype(jnp.float32) + forward_weight[0][:, None] * mixed).astype(jnp.bfloat16)

    back_far = swap_half(dot_last(backward_rows, down[near:]).astype(jnp.bfloat16))

    def back_of(back_r, gate, upper):
        gate, upper = gate.astype(jnp.float32), upper.astype(jnp.float32)
        sigma = jax.nn.sigmoid(gate)
        active = gate * sigma
        saved_hidden = (active * upper).astype(jnp.bfloat16).astype(jnp.float32)
        share = jnp.sum(back_r * saved_hidden, axis=1)
        d_gate = (back_r * upper * sigma * (1.0 + gate * (1.0 - sigma))).astype(jnp.bfloat16)
        d_up = (back_r * active).astype(jnp.bfloat16)
        return jnp.concatenate([d_gate, d_up], axis=1), share

    far_terms, far_share = back_of(back_far.astype(jnp.float32), g[slots:], u[slots:])
    far_terms, backward_rows = lax.optimization_barrier((far_terms, backward_rows))
    middle = gates.shape[0] * 2 // 7 // 128 * 128
    far_part = jnp.concatenate(
        [swap_half(dot_last(far_terms, rows).astype(jnp.bfloat16)) for rows in (gates[:middle], gates[middle:])], axis=1
    )
    far_share = swap_half(far_share)
    near_terms, near_share = back_of(dot_last(backward_rows, down[:near]), g[:slots], u[:slots])
    near_part = dot_last(near_terms, gates)
    part = (near_part + far_part.astype(jnp.float32)).astype(jnp.bfloat16)
    rest, terms = near_share + far_share, []
    for _ in range(3):
        terms.append(rest.astype(jnp.bfloat16))
        rest = rest - terms[-1].astype(jnp.float32)
    width = part.shape[1]
    column = jnp.arange(128, dtype=jnp.int32)[None, :]
    tail = sum(jnp.where(column == n, term[:, None], jnp.bfloat16(0)) for n, term in enumerate(terms))
    returned = exchange(jnp.concatenate([part, tail], axis=1), planes)
    mixed = unpack(returned, backward_keys)
    weight_gradient = jnp.sum(mixed[:, width:], axis=1)
    mixed = mixed[:, :width]
    input_gradient = (upstream.astype(jnp.float32) + backward_weight[0][:, None] * mixed).astype(jnp.bfloat16)
    return (forward_output[None], input_gradient[None], weight_gradient[None])


def solution(mesh):
    placed = (
        P("pipe", "expert", None),
        P("pipe", "expert", None),
        P("pipe", "expert"),
        P("pipe", "expert", None),
        P("pipe", "expert", None),
        P("pipe", "expert"),
        P("pipe", "expert", None, None, None),
        P("pipe", "expert", None, None, None),
        P("pipe", "expert", None, None),
        P("pipe", "expert", None, None),
        P("pipe", "expert", None, None),
    )
    return jax.shard_map(
        per_device,
        mesh=mesh,
        in_specs=placed,
        out_specs=(P("pipe", "expert", None), P("pipe", "expert", None), P("pipe", "expert")),
        check_vma=False,
    )
```
